32 devices in a mesh: dp: 8 (over z, x), comp: 4 (over y, core).
Axes of the slice: x: 2, y: 2, z: 4, core: 2. Of those that a mesh axis runs over, the one named last changes fastest.
Arguments:
- climate_vector: bfloat16 [8, 4, 360, 256], P('dp', 'comp'), may hold values from -6 to 6
- pelagic_vector: bfloat16 [8, 8, 720, 128], P('dp', None, 'comp'), may hold values from -6 to 6
- wet_land_flags: int32 [8, 720], P(None, 'comp'), may hold values 0 or 1
- sky_convolution_weights: bfloat16 [9, 256, 256], replicated, may hold values from -0.125 to 0.125
- pelagic_convolution_weights: bfloat16 [9, 128, 128], replicated, may hold values from -0.1875 to 0.1875
- interface_emission_map: bfloat16 [256, 128], replicated, may hold values from -0.375 to 0.375
- thermal_drive_linear_map: bfloat16 [128, 256], replicated, may hold values from -0.5 to 0.5
- regrid_donor_ids: int32 [8, 720, 4], P('comp'), may hold values from 0 to 1439, as said below
- regrid_donor_factors: float32 [8, 720, 4], P('comp'), as said below
- thermal_donor_ids: int32 [4, 360, 4], P('comp'), may hold values from 0 to 5759, as said below
- thermal_donor_factors: float32 [4, 360, 4], P('comp'), as said below
- upcoming_sky_sensitivity: bfloat16 [8, 4, 360, 256], P('dp', 'comp'), may hold values from -6 to 6
- upcoming_pelagic_sensitivity: bfloat16 [8, 8, 720, 128], P('dp', None, 'comp'), may hold values from -6 to 6
Outputs:
- atmos_next: float32 [8, 4, 360, 256], P('dp', 'comp')
- ocean_next: float32 [8, 8, 720, 128], P('dp', None, 'comp')
- atmos_kernel_grad: float32 [9, 256, 256], P(None, 'dp', 'comp')
- ocean_kernel_grad: float32 [9, 128, 128], P(None, 'dp', 'comp')
The draws below stay inside these ranges and needn't reach their ends.
Inputs may be any that keep to these rules, and one draw needn't show every extreme that they name: `regrid_donor_ids`: the sources of ocean cell (r, j) are atmosphere cells in the same band of 1 row as row r // 2, within one longitude of j // 2, cyclically. `regrid_donor_factors`: positive; the 4 shares of a cell sum to one. `thermal_donor_ids`: the sources of atmosphere cell (r, l) are ocean cells in rows 2r or 2r + 1 and longitudes 2l - 1 to 2l + 2, cyclically. `thermal_donor_factors`: positive; the 4 shares of a cell sum to one.
All inputs are finite; a program needn't handle non-finite values. No bound on the sum of `wet_land_flags` on one device may be relied on, other than what follows from the above.
Results may differ from the reference program's by a relative error of at most 0.004.
Values may be sent and summed in bfloat16 or wider, within the bound.
A program may use at most 64 MiB of HBM per device.

```python
import jax
import jax.numpy as jnp
from jax import lax

ATMOS_CHANNELS = 256
SEAWARD_DEPTHS = 128
ATMOS_LONGITUDES = 360
NEAR = 4
ALAT_DEV = 1
SAMPLES = 8
ATMOS_LATITUDES = 4
OLAT = 8
OLON = 720


def share_draw(key, shape):
    raw = jax.random.uniform(key, shape, jnp.float32, 0.25, 1.0)
    return raw / jnp.sum(raw, axis=-1, keepdims=True)


def draw_regrid_donor_ids(key, part):
    key_row, key_col = jax.random.split(jax.random.fold_in(key, 11))
    rows = jnp.arange(OLAT, dtype=jnp.int32)[:, None, None]
    cols = jnp.arange(OLON, dtype=jnp.int32)[None, :, None]
    centre = rows // 2
    band_start = centre // ALAT_DEV * ALAT_DEV
    row_pick = centre + jax.random.randint(key_row, (OLAT, OLON, NEAR), -1, 2)
    row_pick = jnp.clip(row_pick, band_start, band_start + ALAT_DEV - 1)
    col_pick = (cols // 2 + jax.random.randint(key_col, (OLAT, OLON, NEAR), -1, 2)) % ATMOS_LONGITUDES
    return (row_pick * ATMOS_LONGITUDES + col_pick).astype(jnp.int32)


def draw_regrid_donor_factors(key, part):
    return share_draw(jax.random.fold_in(key, 12), (OLAT, OLON, NEAR))


def draw_thermal_donor_ids(key, part):
    key_row, key_col = jax.random.split(jax.random.fold_in(key, 13))
    rows = jnp.arange(ATMOS_LATITUDES, dtype=jnp.int32)[:, None, None]
    cols = jnp.arange(ATMOS_LONGITUDES, dtype=jnp.int32)[None, :, None]
    row_pick = 2 * rows + jax.random.randint(key_row, (ATMOS_LATITUDES, ATMOS_LONGITUDES, NEAR), 0, 2)
    col_pick = (2 * cols + jax.random.randint(key_col, (ATMOS_LATITUDES, ATMOS_LONGITUDES, NEAR), -1, 3)) % OLON
    return (row_pick * OLON + col_pick).astype(jnp.int32)


def draw_thermal_donor_factors(key, part):
    return share_draw(jax.random.fold_in(key, 14), (ATMOS_LATITUDES, ATMOS_LONGITUDES, NEAR))


def set_ends(entries, key, low, largest):
    index_at = [jax.random.randint(jax.random.fold_in(key, axis), (), 0, length) for axis, length in enumerate(entries.shape)]
    main_axis = entries.shape.index(max(entries.shape))
    neighbour = index_at[:main_axis] + [(index_at[main_axis] + 1) % entries.shape[main_axis]] + index_at[main_axis + 1:]
    return entries.at[tuple(index_at)].set(low).at[tuple(neighbour)].set(largest)


def with_spikes(drawn, key, source, target, shards_of, factor):
    owner, partner = [(jnp.arange(drawn.shape[position]) // (drawn.shape[position] // shards_of)).reshape([-1 if axis == position else 1 for axis in range(drawn.ndim)]) for position in (source, target)]
    chosen = jax.random.permutation(key, shards_of)[partner]
    strong = (owner == chosen) | (owner == (partner + shards_of // 2) % shards_of)
    return jnp.where(strong, factor * drawn, drawn)


def steps_of(rng, shape, pieces, smallest, largest):
    level, own = 1.0, jax.random.fold_in(rng, 6)
    for position, blocks in pieces:
        draws = jnp.exp(jax.random.uniform(jax.random.fold_in(own, position), (blocks,), jnp.float32, smallest / len(pieces), largest / len(pieces)))
        level = level * jnp.repeat(draws, shape[position] // blocks).reshape([-1 if axis == position else 1 for axis in range(len(shape))])
    return level


def gaussian(own_key, extent, scale, reach, cuts=(), kind=jnp.bfloat16):
    values = jax.random.normal(own_key, extent, jnp.float32) * scale
    if len(cuts) > 0:
        values = steps_of(own_key, extent, cuts, -0.22, 0.18) * values
    return jnp.clip(values, min=-reach, max=reach).astype(kind)


def heavy_noise(rng, shape, scale, reach, shards, heavy, held_as=jnp.bfloat16):
    entries = scale * jax.random.normal(rng, shape, jnp.float32)
    if shards:
        entries = entries * steps_of(rng, shape, shards, -0.22, 0.18)
    return jnp.clip(with_spikes(entries, jax.random.fold_in(rng, 3), *heavy), -reach, reach).astype(held_as)


def setup_inputs(seed: int = 0) -> dict:
    splits = jax.random.split(jax.random.key(seed), 14)
    climate_vector = gaussian(splits[0], (SAMPLES, ATMOS_LATITUDES, ATMOS_LONGITUDES, ATMOS_CHANNELS), 1.0, 6.0, ((0, 8), (1, 4)))
    pelagic_vector = gaussian(splits[1], (SAMPLES, OLAT, OLON, SEAWARD_DEPTHS), 1.0, 6.0, ((0, 8), (2, 4)))
    wet_land_flags = set_ends((jax.random.randint(splits[2], (OLAT, OLON), 0, 3) < 2).astype(jnp.int32), jax.random.fold_in(splits[2], 1), 0, 1)
    sky_convolution_weights = gaussian(splits[3], (9, ATMOS_CHANNELS, ATMOS_CHANNELS), (9 * ATMOS_CHANNELS) ** -0.5, 0.125)
    pelagic_convolution_weights = gaussian(splits[4], (9, SEAWARD_DEPTHS, SEAWARD_DEPTHS), (9 * SEAWARD_DEPTHS) ** -0.5, 0.1875)
    interface_emission_map = gaussian(splits[5], (ATMOS_CHANNELS, SEAWARD_DEPTHS), ATMOS_CHANNELS ** -0.5, 0.375)
    thermal_drive_linear_map = gaussian(splits[6], (SEAWARD_DEPTHS, ATMOS_CHANNELS), SEAWARD_DEPTHS ** -0.5, 0.5)
    regrid_donor_ids = draw_regrid_donor_ids(jax.random.fold_in(splits[13], 71), 0)
    regrid_donor_factors = draw_regrid_donor_factors(jax.random.fold_in(splits[13], 71), 0)
    thermal_donor_ids = draw_thermal_donor_ids(jax.random.fold_in(splits[13], 71), 0)
    thermal_donor_factors = draw_thermal_donor_factors(jax.random.fold_in(splits[13], 71), 0)
    upcoming_sky_sensitivity = heavy_noise(splits[11], (SAMPLES, ATMOS_LATITUDES, ATMOS_LONGITUDES, ATMOS_CHANNELS), 1.0, 6.0, ((0, 8), (1, 4)), (0, 3, 8, 2.0))
    upcoming_pelagic_sensitivity = heavy_noise(splits[12], (SAMPLES, OLAT, OLON, SEAWARD_DEPTHS), 1.0, 6.0, ((0, 8), (2, 4)), (0, 3, 8, 2.0))
    return dict(climate_vector=climate_vector, pelagic_vector=pelagic_vector, wet_land_flags=wet_land_flags, sky_convolution_weights=sky_convolution_weights, pelagic_convolution_weights=pelagic_convolution_weights, interface_emission_map=interface_emission_map, thermal_drive_linear_map=thermal_drive_linear_map, regrid_donor_ids=regrid_donor_ids, regrid_donor_factors=regrid_donor_factors, thermal_donor_ids=thermal_donor_ids, thermal_donor_factors=thermal_donor_factors, upcoming_sky_sensitivity=upcoming_sky_sensitivity, upcoming_pelagic_sensitivity=upcoming_pelagic_sensitivity)


def wrap_pad(field):
    padded = jnp.pad(field, ((1, 1), (0, 0), (0, 0)))
    return jnp.concatenate([padded[:, -1:], padded, padded[:, :1]], axis=1)


def convolve(padded, kernel):
    rows = padded.shape[0] - 2
    cols = padded.shape[1] - 2
    width = padded.shape[2]
    total = jnp.zeros((rows * cols, kernel.shape[2]), jnp.float32)
    for tap_row in range(3):
        for tap_col in range(3):
            window = padded[tap_row:tap_row + rows, tap_col:tap_col + cols].reshape(-1, width)
            total = total + jnp.dot(window, kernel[3 * tap_row + tap_col], preferred_element_type=jnp.float32)
    return total.reshape(rows, cols, -1)


def kernel_terms(padded, delta):
    rows = padded.shape[0] - 2
    cols = padded.shape[1] - 2
    width = padded.shape[2]
    flat_delta = delta.reshape(-1, delta.shape[-1])
    taps = []
    for tap_row in range(3):
        for tap_col in range(3):
            window = padded[tap_row:tap_row + rows, tap_col:tap_col + cols].reshape(-1, width)
            taps.append(jnp.dot(window.T, flat_delta, preferred_element_type=jnp.float32))
    return jnp.stack(taps)


def silu_slope(value):
    logistic = jax.nn.sigmoid(value)
    return logistic * (1.0 + value * (1.0 - logistic))


def reference(climate_vector, pelagic_vector, wet_land_flags, sky_convolution_weights, pelagic_convolution_weights, interface_emission_map, thermal_drive_linear_map, regrid_donor_ids, regrid_donor_factors, thermal_donor_ids, thermal_donor_factors, upcoming_sky_sensitivity, upcoming_pelagic_sensitivity):
    wet = wet_land_flags.astype(jnp.float32)[:, :, None]

    def one_sample(carry, inputs):
        atmos_one, solitary_pelagic_vector, cot_a, cot_o = inputs
        flux_cells = jnp.dot(atmos_one.reshape(-1, ATMOS_CHANNELS), interface_emission_map, preferred_element_type=jnp.float32).astype(jnp.bfloat16)
        flux_taken = flux_cells[regrid_donor_ids].astype(jnp.float32)
        flux_ocean = jnp.sum(flux_taken * regrid_donor_factors[..., None], axis=2).astype(jnp.bfloat16)
        pelagic_picked_sites = solitary_pelagic_vector.reshape(-1, SEAWARD_DEPTHS)[thermal_donor_ids].astype(jnp.float32)
        interface_coupling_terms = jnp.sum(pelagic_picked_sites * thermal_donor_factors[..., None], axis=2).astype(jnp.bfloat16)
        atmosphere_forcing = jnp.dot(interface_coupling_terms.reshape(-1, SEAWARD_DEPTHS), thermal_drive_linear_map, preferred_element_type=jnp.float32).reshape(ATMOS_LATITUDES, ATMOS_LONGITUDES, ATMOS_CHANNELS)
        padded_a = wrap_pad(atmos_one)
        za = convolve(padded_a, sky_convolution_weights) + atmosphere_forcing
        next_a = atmos_one.astype(jnp.float32) + jax.nn.silu(za)
        padded_o = wrap_pad(solitary_pelagic_vector)
        zo = convolve(padded_o, pelagic_convolution_weights) + flux_ocean.astype(jnp.float32)
        next_o = solitary_pelagic_vector.astype(jnp.float32) + wet * jax.nn.silu(zo)
        delta_a = (cot_a.astype(jnp.float32) * silu_slope(za)).astype(jnp.bfloat16)
        delta_o = (cot_o.astype(jnp.float32) * wet * silu_slope(zo)).astype(jnp.bfloat16)
        grad_a = carry[0] + kernel_terms(padded_a, delta_a)
        grad_o = carry[1] + kernel_terms(padded_o, delta_o)
        return (grad_a, grad_o), (next_a, next_o)

    start = (jnp.zeros((9, ATMOS_CHANNELS, ATMOS_CHANNELS), jnp.float32), jnp.zeros((9, SEAWARD_DEPTHS, SEAWARD_DEPTHS), jnp.float32))
    grads, states = lax.scan(one_sample, start, (climate_vector, pelagic_vector, upcoming_sky_sensitivity, upcoming_pelagic_sensitivity))
    return states[0], states[1], grads[0], grads[1]
```

```python
import functools

import jax
import jax.numpy as jnp
from jax import lax
from jax.experimental import pallas as pl
from jax.experimental.pallas import tpu as pltpu
from jax.sharding import PartitionSpec as P


def with_halo(cells, sides, width, closed):
    for axis, dim in sides:
        count = lax.axis_size(axis)
        ends = count if closed else count - 1
        head = lax.slice_in_dim(cells, 0, width, axis=dim)
        tail = lax.slice_in_dim(cells, cells.shape[dim] - width, cells.shape[dim], axis=dim)
        cells = jnp.concatenate(
            [
                lax.ppermute(tail, axis, [(i, (i + 1) % count) for i in range(ends)]),
                cells,
                lax.ppermute(head, axis, [((i + 1) % count, i) for i in range(ends)]),
            ],
            axis=dim,
        )
    return cells


def convolve(padded, kernel):
    sample_batch = padded.shape[0]
    rows = padded.shape[1] - 2
    cols = padded.shape[2] - 2
    width = padded.shape[3]
    total = jnp.zeros((sample_batch * rows * cols, kernel.shape[2]), jnp.float32)
    for tap_row in range(3):
        for tap_col in range(3):
            window = padded[:, tap_row : tap_row + rows, tap_col : tap_col + cols].reshape(
                -1, width
            )
            total = total + jnp.dot(
                window, kernel[3 * tap_row + tap_col], preferred_element_type=jnp.float32
            )
    return total.reshape(sample_batch, rows, cols, -1)


MESH = pl.DeviceIdType.MESH


def joined_terms(padded, delta):
    rows = padded.shape[1] - 2
    cols = padded.shape[2] - 2
    flat_delta = delta.reshape(-1, delta.shape[-1])
    joined = jnp.concatenate([padded[:, :, b : b + cols] for b in range(3)], axis=-1)
    return jnp.stack(
        [
            lax.dot_general(
                flat_delta,
                joined[:, a : a + rows].reshape(-1, joined.shape[-1]),
                (((0,), (0,)), ((), ())),
                preferred_element_type=jnp.float32,
            )
            for a in range(3)
        ]
    )


def remote(src, dst, sems, index, target):
    return pltpu.make_async_remote_copy(
        src_ref=src,
        dst_ref=dst,
        send_sem=sems.at[0, index],
        recv_sem=sems.at[1, index],
        device_id=target,
        device_id_type=MESH,
    )


def reduce_kernel(
    samples, ga_ref, go_ref, outa_ref, outo_ref, r1a, r1o, s2a, s2o, r2a, r2o, da, r4, sems
):
    comp = lax.axis_index("comp")
    dp = lax.axis_index("dp")
    core = lax.rem(comp, 2)
    half = comp // 2
    twin = {"comp": 2 * half + 1 - core}
    across = {"comp": 2 * (1 - half) + core}
    barrier = pltpu.get_barrier_semaphore()
    pl.semaphore_signal(barrier, inc=1, device_id=twin, device_id_type=MESH)
    pl.semaphore_signal(barrier, inc=1, device_id=across, device_id_type=MESH)
    for k in range(1, samples):
        pl.semaphore_signal(
            barrier, inc=1, device_id={"dp": lax.rem(dp + k, samples)}, device_id_type=MESH
        )
    pl.semaphore_wait(barrier, samples + 1)
    wa = s2a.shape[1]
    wo = s2o.shape[1]

    def block(ref, width, band):
        return ref.at[:, pl.ds(pl.multiple_of(band * width, width), width), :]

    first = []
    for n, side in enumerate((1 - half, half)):
        band = 2 * side + 1 - core
        first.append(
            (
                remote(block(ga_ref, wa, band), r1a.at[n], sems, 2 * n, twin),
                remote(block(go_ref, wo, band), r1o.at[n], sems, 2 * n + 1, twin),
            )
        )
    for pair in first:
        for copy in pair:
            copy.start()
    other = 2 * (1 - half) + core
    first[0][0].wait_recv()
    s2a[...] = (
        block(ga_ref, wa, other)[...].astype(jnp.float32) + r1a[0].astype(jnp.float32)
    ).astype(jnp.bfloat16)
    second_a = remote(s2a, r2a, sems, 4, across)
    second_a.start()
    first[0][1].wait_recv()
    s2o[...] = (
        block(go_ref, wo, other)[...].astype(jnp.float32) + r1o[0].astype(jnp.float32)
    ).astype(jnp.bfloat16)
    second_o = remote(s2o, r2o, sems, 5, across)
    second_o.start()
    first[1][0].wait_recv()
    first[1][1].wait_recv()
    own_a = block(ga_ref, wa, comp)[...].astype(jnp.float32) + r1a[1].astype(jnp.float32)
    own_o = block(go_ref, wo, comp)[...].astype(jnp.float32) + r1o[1].astype(jnp.float32)
    second_a.wait_recv()
    own_a = own_a + r2a[...].astype(jnp.float32)
    second_o.wait_recv()
    own_o = own_o + r2o[...].astype(jnp.float32)
    ca = outa_ref.shape[1]
    co = outo_ref.shape[1]
    ta = own_a.reshape(3 * wa, -1)
    ta = jnp.concatenate([ta, jnp.zeros((wa, ta.shape[1]), jnp.float32)], axis=0).T
    to = own_o.reshape(3 * wo, -1)
    to = jnp.concatenate([to, jnp.zeros((wo, to.shape[1]), jnp.float32)], axis=0).T
    ta = ta.astype(jnp.bfloat16)
    to = to.astype(jnp.bfloat16)
    for d in range(samples):
        for b in range(3):
            piece = ta[(b * samples + d) * ca : (b * samples + d + 1) * ca]
            da[d, b * ca : (b + 1) * ca, :] = piece[:, :128]
            da[d, (3 + b) * ca : (4 + b) * ca, :] = piece[:, 128:]
            da[d, 6 * ca + b * co : 6 * ca + (b + 1) * co, :] = to[
                (b * samples + d) * co : (b * samples + d + 1) * co
            ]
    third = []
    for k in range(1, samples):
        peer = lax.rem(dp + k, samples)
        copy = remote(da.at[peer], r4.at[k - 1], sems, 5 + k, {"dp": peer})
        copy.start()
        third.append(copy)
    total = da[dp].astype(jnp.float32)
    for copy, k in zip(third, range(samples)):
        copy.wait_recv()
        total = total + r4[k].astype(jnp.float32)
    for a in range(3):
        for b in range(3):
            row = b * ca + (a // 2) * 3 * ca
            outa_ref[3 * a + b] = total[row : row + ca, (a % 2) * wa : (a % 2 + 1) * wa]
            row = 6 * ca + b * co
            outo_ref[3 * a + b] = total[row : row + co, a * wo : (a + 1) * wo]
    for pair in first:
        for copy in pair:
            copy.wait_send()
    second_a.wait_send()
    second_o.wait_send()
    for copy in third:
        copy.wait_send()


def plain_sum(joined):
    width = joined.shape[2] // 3
    terms = joined.reshape(3, -1, 3, width).transpose(0, 2, 3, 1).reshape(9, width, -1)
    banded = lax.psum_scatter(terms, "comp", scatter_dimension=2, tiled=True)
    return lax.psum_scatter(banded, "dp", scatter_dimension=1, tiled=True)


def summed_terms(ga, go):
    samples = lax.axis_size("dp")
    bands = lax.axis_size("comp")
    wa, wo = ga.shape[1] // bands, go.shape[1] // bands
    ca, co = ga.shape[2] // 3 // samples, go.shape[2] // 3 // samples
    if bands != 4 or wa != 64 or wo != 32 or ca % 16 or co % 16:
        return plain_sum(ga), plain_sum(go)
    la, lo = ga.shape[2], go.shape[2]
    piece = 6 * ca + 3 * co
    vmem = pl.BlockSpec(memory_space=pltpu.VMEM)
    return pl.pallas_call(
        functools.partial(reduce_kernel, samples),
        out_shape=(
            jax.ShapeDtypeStruct((9, ca, wa), jnp.float32),
            jax.ShapeDtypeStruct((9, co, wo), jnp.float32),
        ),
        in_specs=[vmem] * 2,
        out_specs=(vmem, vmem),
        scratch_shapes=[
            pltpu.VMEM((2, 3, wa, la), jnp.bfloat16),
            pltpu.VMEM((2, 3, wo, lo), jnp.bfloat16),
            pltpu.VMEM((3, wa, la), jnp.bfloat16),
            pltpu.VMEM((3, wo, lo), jnp.bfloat16),
            pltpu.VMEM((3, wa, la), jnp.bfloat16),
            pltpu.VMEM((3, wo, lo), jnp.bfloat16),
            pltpu.VMEM((samples, piece, 128), jnp.bfloat16),
            pltpu.VMEM((samples - 1, piece, 128), jnp.bfloat16),
            pltpu.SemaphoreType.DMA((2, 5 + samples)),
        ],
        compiler_params=pltpu.CompilerParams(
            collective_id=0, has_side_effects=True, vmem_limit_bytes=32 * 1024 * 1024
        ),
    )(ga.astype(jnp.bfloat16), go.astype(jnp.bfloat16))


def silu_slope(value):
    logistic = jax.nn.sigmoid(value)
    return logistic * (1.0 + value * (1.0 - logistic))


def per_device(
    climate_vector,
    pelagic_vector,
    wet_land_flags,
    sky_convolution_weights,
    pelagic_convolution_weights,
    interface_emission_map,
    thermal_drive_linear_map,
    regrid_donor_ids,
    regrid_donor_factors,
    thermal_donor_ids,
    thermal_donor_factors,
    upcoming_sky_sensitivity,
    upcoming_pelagic_sensitivity,
):
    sample_batch, band_rows, atmos_lons, atmos_width = climate_vector.shape
    ocean_rows, band_lons, ocean_grid_width = (
        pelagic_vector.shape[1],
        pelagic_vector.shape[2],
        pelagic_vector.shape[3],
    )
    bands = lax.axis_size("comp")
    parallel_slice = lax.axis_index("comp")
    coupled_entry_pairs = 2 * band_rows
    pelagic_east_total = band_lons * bands
    near = regrid_donor_ids.shape[2]
    ocean_blocks = pelagic_vector.reshape(
        sample_batch, bands, coupled_entry_pairs, band_lons, ocean_grid_width
    )
    surface_exchange_input = lax.all_to_all(
        ocean_blocks, "comp", split_axis=1, concat_axis=1, tiled=True
    )
    flux_cells = jnp.dot(
        climate_vector.reshape(-1, atmos_width),
        interface_emission_map,
        preferred_element_type=jnp.float32,
    )
    flux_cells = flux_cells.astype(jnp.bfloat16)
    cells_flat = flux_cells.reshape(sample_batch, band_rows * atmos_lons, ocean_grid_width)
    local_flux = regrid_donor_ids - parallel_slice * (band_rows * atmos_lons)
    local_flux = local_flux.reshape(coupled_entry_pairs, bands, band_lons, near).transpose(
        1, 0, 2, 3
    )
    flux_weights = regrid_donor_factors.reshape(
        coupled_entry_pairs, bands, band_lons, near
    ).transpose(1, 0, 2, 3)
    flux_taken = jnp.take(cells_flat, local_flux, axis=1).astype(jnp.float32)
    flux_send = jnp.sum(flux_taken * flux_weights[None, ..., None], axis=4).astype(jnp.bfloat16)
    flux_in = lax.all_to_all(flux_send, "comp", split_axis=1, concat_axis=1, tiled=True)
    padded_a = with_halo(climate_vector, (("comp", 1),), 1, False)
    padded_a = jnp.concatenate([padded_a[:, :, -1:], padded_a, padded_a[:, :, :1]], axis=2)
    conv_a = convolve(padded_a, sky_convolution_weights)
    padded_o = with_halo(pelagic_vector, (("comp", 2),), 1, True)
    padded_o = jnp.pad(padded_o, ((0, 0), (1, 1), (0, 0), (0, 0)))
    conv_o = convolve(padded_o, pelagic_convolution_weights)
    source_row_index = (
        thermal_donor_ids // pelagic_east_total - parallel_slice * coupled_entry_pairs
    )
    donor_east_ids = thermal_donor_ids % pelagic_east_total
    nearby_thermal_values = (
        donor_east_ids // band_lons * coupled_entry_pairs + source_row_index
    ) * band_lons + donor_east_ids % band_lons
    pelagic_picked_sites = jnp.take(
        surface_exchange_input.reshape(sample_batch, -1, ocean_grid_width),
        nearby_thermal_values,
        axis=1,
    ).astype(jnp.float32)
    interface_coupling_terms = jnp.sum(
        pelagic_picked_sites * thermal_donor_factors[None, ..., None], axis=3
    ).astype(jnp.bfloat16)
    atmosphere_forcing = jnp.dot(
        interface_coupling_terms.reshape(-1, ocean_grid_width),
        thermal_drive_linear_map,
        preferred_element_type=jnp.float32,
    )
    za = conv_a + atmosphere_forcing.reshape(sample_batch, band_rows, atmos_lons, atmos_width)
    atmos_next = climate_vector.astype(jnp.float32) + jax.nn.silu(za)
    flux_ocean = flux_in.reshape(sample_batch, ocean_rows, band_lons, ocean_grid_width)
    wet = wet_land_flags.astype(jnp.float32)[None, :, :, None]
    zo = conv_o + flux_ocean.astype(jnp.float32)
    ocean_next = pelagic_vector.astype(jnp.float32) + wet * jax.nn.silu(zo)
    delta_a = (upcoming_sky_sensitivity.astype(jnp.float32) * silu_slope(za)).astype(jnp.bfloat16)
    delta_o = (upcoming_pelagic_sensitivity.astype(jnp.float32) * wet * silu_slope(zo)).astype(
        jnp.bfloat16
    )
    summed = summed_terms(joined_terms(padded_a, delta_a), joined_terms(padded_o, delta_o))
    return (atmos_next, ocean_next, summed[0], summed[1])


def solution(mesh):
    placed = (
        P("dp", "comp", None, None),
        P("dp", None, "comp", None),
        P(None, "comp"),
        P(),
        P(),
        P(),
        P(),
        P("comp", None, None),
        P("comp", None, None),
        P("comp", None, None),
        P("comp", None, None),
        P("dp", "comp", None, None),
        P("dp", None, "comp", None),
    )
    return jax.shard_map(
        per_device,
        mesh=mesh,
        in_specs=placed,
        out_specs=(
            P("dp", "comp", None, None),
            P("dp", None, "comp", None),
            P(None, "dp", "comp"),
            P(None, "dp", "comp"),
        ),
        check_vma=False,
    )
```

```python
import functools

import jax
import jax.numpy as jnp
from jax import lax
from jax.experimental import pallas as pl
from jax.experimental.pallas import tpu as pltpu
from jax.sharding import PartitionSpec as P


def with_halo(cells, sides, width, closed):
    for axis, dim in sides:
        count = lax.axis_size(axis)
        ends = count if closed else count - 1
        head = lax.slice_in_dim(cells, 0, width, axis=dim)
        tail = lax.slice_in_dim(cells, cells.shape[dim] - width, cells.shape[dim], axis=dim)
        cells = jnp.concatenate(
            [
                lax.ppermute(tail, axis, [(i, (i + 1) % count) for i in range(ends)]),
                cells,
                lax.ppermute(head, axis, [((i + 1) % count, i) for i in range(ends)]),
            ],
            axis=dim,
        )
    return cells


def convolve(padded, kernel):
    sample_batch = padded.shape[0]
    rows = padded.shape[1] - 2
    cols = padded.shape[2] - 2
    width = padded.shape[3]
    total = jnp.zeros((sample_batch * rows * cols, kernel.shape[2]), jnp.float32)
    for tap_row in range(3):
        for tap_col in range(3):
            window = padded[:, tap_row : tap_row + rows, tap_col : tap_col + cols].reshape(
                -1, width
            )
            total = total + jnp.dot(
                window, kernel[3 * tap_row + tap_col], preferred_element_type=jnp.float32
            )
    return total.reshape(sample_batch, rows, cols, -1)


MESH = pl.DeviceIdType.MESH


def joined_terms(padded, delta):
    rows = padded.shape[1] - 2
    cols = padded.shape[2] - 2
    flat_delta = delta.reshape(-1, delta.shape[-1])
    joined = jnp.concatenate([padded[:, :, b : b + cols] for b in range(3)], axis=-1)
    return jnp.stack(
        [
            lax.dot_general(
                flat_delta,
                joined[:, a : a + rows].reshape(-1, joined.shape[-1]),
                (((0,), (0,)), ((), ())),
                preferred_element_type=jnp.float32,
            )
            for a in range(3)
        ]
    )


def remote(src, dst, sems, index, target):
    return pltpu.make_async_remote_copy(
        src_ref=src,
        dst_ref=dst,
        send_sem=sems.at[0, index],
        recv_sem=sems.at[1, index],
        device_id=target,
        device_id_type=MESH,
    )


def two_parts(value):
    high = value.astype(jnp.bfloat16)
    return high, (value - high.astype(jnp.float32)).astype(jnp.bfloat16)


def picked(ids, factors, first, cells):
    extent = cells.shape[0]
    place = lax.broadcasted_iota(jnp.int32, (extent, ids.shape[1]), 0) + first
    shares = jnp.zeros(place.shape, jnp.float32)
    for k in range(ids.shape[0]):
        shares = shares + jnp.where(place == ids[k : k + 1], factors[k : k + 1], 0.0)
    return sum(turned_dot(part, cells) for part in two_parts(shares))


def turned_dot(left, right):
    return lax.dot_general(
        left, right, (((0,), (0,)), ((), ())), preferred_element_type=jnp.float32
    )


def step_kernel(
    samples,
    x_ref, p_ref, wet_ref, wa_ref, wo_ref, emit_ref, drive_ref,
    rid_ref, rfac_ref, tid_ref, tfac_ref, cota_ref, coto_ref,
    nexta_ref, nexto_ref, outa_ref, outo_ref,
    hal, xo, fs, fi, hs, hr, ax, xca, pp, xco, dea, deo, ga_ref, go_ref,
    r1a, r1o, s2a, s2o, r2a, r2o, da, r4, sems, near,
):
    comp = lax.axis_index("comp")
    dp = lax.axis_index("dp")
    bands = 4
    rows, lons = p_ref.shape[0], p_ref.shape[1]
    cells = x_ref.shape[0]
    core = lax.rem(comp, 2)
    half = comp // 2
    twin = {"comp": 2 * half + 1 - core}
    across = {"comp": 2 * (1 - half) + core}
    barrier = pltpu.get_barrier_semaphore()
    for k in range(1, bands):
        pl.semaphore_signal(
            barrier, inc=1, device_id={"comp": lax.rem(comp + k, bands)}, device_id_type=MESH
        )
    for k in range(1, samples):
        pl.semaphore_signal(
            barrier, inc=1, device_id={"dp": lax.rem(dp + k, samples)}, device_id_type=MESH
        )
    pl.semaphore_wait(barrier, samples + bands - 2)
    up = {"comp": lax.rem(comp + 1, bands)}
    down = {"comp": lax.rem(comp + bands - 1, bands)}
    halos = [
        remote(x_ref, hal.at[0], near, 0, up),
        remote(x_ref, hal.at[1], near, 1, down),
    ]
    swaps = []
    for k in range(1, bands):
        peer = lax.rem(comp + k, bands)
        swaps.append(
            remote(
                p_ref.at[pl.ds(2 * peer, 2)],
                xo.at[pl.ds(2 * comp, 2)],
                near,
                3 + k,
                {"comp": peer},
            )
        )
    for copy in halos + swaps:
        copy.start()
    pp[...] = jnp.zeros_like(pp)
    for r in range(rows):
        pp[r, 8 : 8 + lons, :] = p_ref[r].astype(jnp.float32)
    hs[0] = pp[:, 7 + lons : 8 + lons, :]
    hs[1] = pp[:, 8:9, :]
    sides = [remote(hs.at[0], hr.at[0], near, 2, up), remote(hs.at[1], hr.at[1], near, 3, down)]
    for copy in sides:
        copy.start()
    flux_cells = jnp.dot(
        x_ref[...], emit_ref[...], preferred_element_type=jnp.float32
    ).astype(jnp.bfloat16)
    fluxes = []
    for k in (1, 2, 3, 0):
        peer = lax.rem(comp + k, bands)
        for r in range(2):
            value = picked(
                rid_ref[2 * peer + r], rfac_ref[2 * peer + r], comp * cells, flux_cells
            ).astype(jnp.bfloat16)
            if k:
                fs[2 * (k - 1) + r] = value
            else:
                fi[2 * comp + r] = value
        if k:
            copy = remote(
                fs.at[pl.ds(2 * (k - 1), 2)],
                fi.at[pl.ds(2 * comp, 2)],
                near,
                6 + k,
                {"comp": peer},
            )
            copy.start()
            fluxes.append(copy)
    xo[pl.ds(2 * comp, 2)] = p_ref[pl.ds(2 * comp, 2)]
    wide = x_ref.shape[1]
    xca[...] = jnp.zeros_like(xca)
    dea[...] = jnp.zeros_like(dea)
    xco[...] = jnp.zeros_like(xco)
    deo[...] = jnp.zeros_like(deo)
    for a in (1, 0, 2):
        if a == 1:
            line = x_ref[...].astype(jnp.float32)
        else:
            halos[a // 2].wait_recv()
            line = jnp.where(
                comp == (0 if a == 0 else bands - 1), 0.0, hal[a // 2].astype(jnp.float32)
            )
        ax[8 : 8 + cells, :] = line
        ax[7:8, :] = line[cells - 1 : cells]
        ax[8 + cells : 9 + cells, :] = line[0:1]
        for b in range(3):
            xca[a, 0:cells, b * wide : (b + 1) * wide] = ax[7 + b : 7 + b + cells, :].astype(
                jnp.bfloat16
            )
    za = jnp.dot(xca[0], wa_ref[0], preferred_element_type=jnp.float32)
    za = za + jnp.dot(xca[1], wa_ref[1], preferred_element_type=jnp.float32)
    za = za + jnp.dot(xca[2], wa_ref[2], preferred_element_type=jnp.float32)
    za = za[:cells]
    for copy in swaps:
        copy.wait_recv()
    total_lons = lons * bands
    surface = jnp.zeros((cells, p_ref.shape[2]), jnp.float32)
    for t in range(bands):
        for r in range(2):
            surface = surface + picked(
                tid_ref[...],
                tfac_ref[...],
                (2 * comp + r) * total_lons + t * lons,
                xo[2 * t + r],
            )
    za = za + jnp.dot(
        surface.astype(jnp.bfloat16), drive_ref[...], preferred_element_type=jnp.float32
    )
    gate = lax.logistic(za)
    nexta_ref[...] = x_ref[...].astype(jnp.float32) + za * gate
    dea[0:cells, :] = (
        cota_ref[...].astype(jnp.float32) * (gate * (1.0 + za * (1.0 - gate)))
    ).astype(jnp.bfloat16)
    for a in range(3):
        ga_ref[a] = turned_dot(dea[...], xca[a]).astype(jnp.bfloat16)
    wa = s2a.shape[1]
    wo = s2o.shape[1]

    def block(ref, width, band):
        return ref.at[:, pl.ds(pl.multiple_of(band * width, width), width), :]

    first = []
    for n, side in enumerate((1 - half, half)):
        band = 2 * side + 1 - core
        first.append(
            (
                remote(block(ga_ref, wa, band), r1a.at[n], sems, 2 * n, twin),
                remote(block(go_ref, wo, band), r1o.at[n], sems, 2 * n + 1, twin),
            )
        )
    first[0][0].start()
    first[1][0].start()

    for copy in sides:
        copy.wait_recv()
    pp[:, 7:8, :] = hr[0]
    pp[:, 8 + lons : 9 + lons, :] = hr[1]
    thin = p_ref.shape[2]

    def join(r, carry):
        for b in range(3):
            xco[r + 1, 0:lons, b * thin : (b + 1) * thin] = pp[
                r, 7 + b : 7 + b + lons, :
            ].astype(jnp.bfloat16)
        return carry

    lax.fori_loop(0, rows, join, 0)
    other = 2 * (1 - half) + core
    first[0][0].wait_recv()
    s2a[...] = (
        block(ga_ref, wa, other)[...].astype(jnp.float32) + r1a[0].astype(jnp.float32)
    ).astype(jnp.bfloat16)
    second_a = remote(s2a, r2a, sems, 4, across)
    second_a.start()
    for copy in fluxes:
        copy.wait_recv()

    def ocean(r, carry):
        zo = jnp.dot(xco[r], wo_ref[0], preferred_element_type=jnp.float32)
        zo = zo + jnp.dot(xco[r + 1], wo_ref[1], preferred_element_type=jnp.float32)
        zo = zo + jnp.dot(xco[r + 2], wo_ref[2], preferred_element_type=jnp.float32)
        zo = zo[:lons] + fi[r].astype(jnp.float32)
        chosen = jnp.where(
            lax.broadcasted_iota(jnp.int32, (rows, thin), 0) == r, 1.0, 0.0
        ).astype(jnp.bfloat16)
        wet = turned_dot(wet_ref[...].astype(jnp.float32).astype(jnp.bfloat16), chosen)
        gate = lax.logistic(zo)
        nexto_ref[r] = p_ref[r].astype(jnp.float32) + wet * (zo * gate)
        deo[r, 0:lons, :] = (
            coto_ref[r].astype(jnp.float32) * wet * (gate * (1.0 + zo * (1.0 - gate)))
        ).astype(jnp.bfloat16)
        return carry

    lax.fori_loop(0, rows, ocean, 0)
    delta = deo[...].reshape(-1, thin)
    for a in range(3):
        go_ref[a] = turned_dot(
            delta, xco[a : a + rows].reshape(-1, 3 * thin)
        ).astype(jnp.bfloat16)
    first[0][1].start()
    first[1][1].start()
    first[0][1].wait_recv()
    s2o[...] = (
        block(go_ref, wo, other)[...].astype(jnp.float32) + r1o[0].astype(jnp.float32)
    ).astype(jnp.bfloat16)
    second_o = remote(s2o, r2o, sems, 5, across)
    second_o.start()
    first[1][0].wait_recv()
    first[1][1].wait_recv()
    own_a = block(ga_ref, wa, comp)[...].astype(jnp.float32) + r1a[1].astype(jnp.float32)
    own_o = block(go_ref, wo, comp)[...].astype(jnp.float32) + r1o[1].astype(jnp.float32)
    second_a.wait_recv()
    own_a = own_a + r2a[...].astype(jnp.float32)
    second_o.wait_recv()
    own_o = own_o + r2o[...].astype(jnp.float32)
    ca = outa_ref.shape[1]
    co = outo_ref.shape[1]
    ta = own_a.reshape(3 * wa, -1)
    ta = jnp.concatenate([ta, jnp.zeros((wa, ta.shape[1]), jnp.float32)], axis=0).T
    to = own_o.reshape(3 * wo, -1)
    to = jnp.concatenate([to, jnp.zeros((wo, to.shape[1]), jnp.float32)], axis=0).T
    ta = ta.astype(jnp.bfloat16)
    to = to.astype(jnp.bfloat16)
    for d in range(samples):
        for b in range(3):
            piece = ta[(b * samples + d) * ca : (b * samples + d + 1) * ca]
            da[d, b * ca : (b + 1) * ca, :] = piece[:, :128]
            da[d, (3 + b) * ca : (4 + b) * ca, :] = piece[:, 128:]
            da[d, 6 * ca + b * co : 6 * ca + (b + 1) * co, :] = to[
                (b * samples + d) * co : (b * samples + d + 1) * co
            ]
    third = []
    for k in range(1, samples):
        peer = lax.rem(dp + k, samples)
        copy = remote(da.at[peer], r4.at[k - 1], sems, 5 + k, {"dp": peer})
        copy.start()
        third.append(copy)
    total = da[dp].astype(jnp.float32)
    for copy, k in zip(third, range(samples)):
        copy.wait_recv()
        total = total + r4[k].astype(jnp.float32)
    for a in range(3):
        for b in range(3):
            row = b * ca + (a // 2) * 3 * ca
            outa_ref[3 * a + b] = total[row : row + ca, (a % 2) * wa : (a % 2 + 1) * wa]
            row = 6 * ca + b * co
            outo_ref[3 * a + b] = total[row : row + co, a * wo : (a + 1) * wo]
    for pair in first:
        for copy in pair:
            copy.wait_send()
    second_a.wait_send()
    second_o.wait_send()
    for copy in third:
        copy.wait_send()
    for copy in halos + swaps + sides + fluxes:
        copy.wait_send()


def plain_sum(joined):
    width = joined.shape[2] // 3
    terms = joined.reshape(3, -1, 3, width).transpose(0, 2, 3, 1).reshape(9, width, -1)
    banded = lax.psum_scatter(terms, "comp", scatter_dimension=2, tiled=True)
    return lax.psum_scatter(banded, "dp", scatter_dimension=1, tiled=True)


def silu_slope(value):
    logistic = jax.nn.sigmoid(value)
    return logistic * (1.0 + value * (1.0 - logistic))


def by_parts(
    climate_vector,
    pelagic_vector,
    wet_land_flags,
    sky_convolution_weights,
    pelagic_convolution_weights,
    interface_emission_map,
    thermal_drive_linear_map,
    regrid_donor_ids,
    regrid_donor_factors,
    thermal_donor_ids,
    thermal_donor_factors,
    upcoming_sky_sensitivity,
    upcoming_pelagic_sensitivity,
):
    sample_batch, band_rows, atmos_lons, atmos_width = climate_vector.shape
    ocean_rows, band_lons, ocean_grid_width = (
        pelagic_vector.shape[1],
        pelagic_vector.shape[2],
        pelagic_vector.shape[3],
    )
    bands = lax.axis_size("comp")
    parallel_slice = lax.axis_index("comp")
    coupled_entry_pairs = 2 * band_rows
    pelagic_east_total = band_lons * bands
    near = regrid_donor_ids.shape[2]
    ocean_blocks = pelagic_vector.reshape(
        sample_batch, bands, coupled_entry_pairs, band_lons, ocean_grid_width
    )
    surface_exchange_input = lax.all_to_all(
        ocean_blocks, "comp", split_axis=1, concat_axis=1, tiled=True
    )
    flux_cells = jnp.dot(
        climate_vector.reshape(-1, atmos_width),
        interface_emission_map,
        preferred_element_type=jnp.float32,
    )
    flux_cells = flux_cells.astype(jnp.bfloat16)
    cells_flat = flux_cells.reshape(sample_batch, band_rows * atmos_lons, ocean_grid_width)
    local_flux = regrid_donor_ids - parallel_slice * (band_rows * atmos_lons)
    local_flux = local_flux.reshape(coupled_entry_pairs, bands, band_lons, near).transpose(
        1, 0, 2, 3
    )
    flux_weights = regrid_donor_factors.reshape(
        coupled_entry_pairs, bands, band_lons, near
    ).transpose(1, 0, 2, 3)
    flux_taken = jnp.take(cells_flat, local_flux, axis=1).astype(jnp.float32)
    flux_send = jnp.sum(flux_taken * flux_weights[None, ..., None], axis=4).astype(jnp.bfloat16)
    flux_in = lax.all_to_all(flux_send, "comp", split_axis=1, concat_axis=1, tiled=True)
    padded_a = with_halo(climate_vector, (("comp", 1),), 1, False)
    padded_a = jnp.concatenate([padded_a[:, :, -1:], padded_a, padded_a[:, :, :1]], axis=2)
    conv_a = convolve(padded_a, sky_convolution_weights)
    padded_o = with_halo(pelagic_vector, (("comp", 2),), 1, True)
    padded_o = jnp.pad(padded_o, ((0, 0), (1, 1), (0, 0), (0, 0)))
    conv_o = convolve(padded_o, pelagic_convolution_weights)
    source_row_index = (
        thermal_donor_ids // pelagic_east_total - parallel_slice * coupled_entry_pairs
    )
    donor_east_ids = thermal_donor_ids % pelagic_east_total
    nearby_thermal_values = (
        donor_east_ids // band_lons * coupled_entry_pairs + source_row_index
    ) * band_lons + donor_east_ids % band_lons
    pelagic_picked_sites = jnp.take(
        surface_exchange_input.reshape(sample_batch, -1, ocean_grid_width),
        nearby_thermal_values,
        axis=1,
    ).astype(jnp.float32)
    interface_coupling_terms = jnp.sum(
        pelagic_picked_sites * thermal_donor_factors[None, ..., None], axis=3
    ).astype(jnp.bfloat16)
    atmosphere_forcing = jnp.dot(
        interface_coupling_terms.reshape(-1, ocean_grid_width),
        thermal_drive_linear_map,
        preferred_element_type=jnp.float32,
    )
    za = conv_a + atmosphere_forcing.reshape(sample_batch, band_rows, atmos_lons, atmos_width)
    atmos_next = climate_vector.astype(jnp.float32) + jax.nn.silu(za)
    flux_ocean = flux_in.reshape(sample_batch, ocean_rows, band_lons, ocean_grid_width)
    wet = wet_land_flags.astype(jnp.float32)[None, :, :, None]
    zo = conv_o + flux_ocean.astype(jnp.float32)
    ocean_next = pelagic_vector.astype(jnp.float32) + wet * jax.nn.silu(zo)
    delta_a = (upcoming_sky_sensitivity.astype(jnp.float32) * silu_slope(za)).astype(jnp.bfloat16)
    delta_o = (upcoming_pelagic_sensitivity.astype(jnp.float32) * wet * silu_slope(zo)).astype(
        jnp.bfloat16
    )
    summed = (
        plain_sum(joined_terms(padded_a, delta_a)),
        plain_sum(joined_terms(padded_o, delta_o)),
    )
    return (atmos_next, ocean_next, summed[0], summed[1])


def whole_step(x, p, wet, wa, wo, emit, drive, rid, rfac, tid, tfac, cota, coto):
    samples = lax.axis_size("dp")
    bands = lax.axis_size("comp")
    rows, lons, thin = p.shape[1:]
    cells, wide = x.shape[2:]
    ca, co, va, vo = wide // samples, thin // samples, wide // bands, thin // bands
    tall = -(-lons // 64) * 64
    high = -(-cells // 128) * 128
    near = rid.shape[2]

    def by_band(ids):
        return ids.reshape(2, bands, lons, near).transpose(1, 0, 3, 2).reshape(-1, near, lons)

    vmem = pl.BlockSpec(memory_space=pltpu.VMEM)
    half, full = jnp.bfloat16, jnp.float32
    piece = 6 * ca + 3 * co
    outs = pl.pallas_call(
        functools.partial(step_kernel, samples),
        out_shape=(
            jax.ShapeDtypeStruct((cells, wide), full),
            jax.ShapeDtypeStruct((rows, lons, thin), full),
            jax.ShapeDtypeStruct((9, ca, va), full),
            jax.ShapeDtypeStruct((9, co, vo), full),
        ),
        in_specs=[vmem] * 13,
        out_specs=(vmem,) * 4,
        scratch_shapes=[
            pltpu.VMEM((2, cells, wide), half),
            pltpu.VMEM((rows, lons, thin), half),
            pltpu.VMEM((2 * bands - 2, lons, thin), half),
            pltpu.VMEM((rows, lons, thin), half),
            pltpu.VMEM((2, rows, 1, thin), full),
            pltpu.VMEM((2, rows, 1, thin), full),
            pltpu.VMEM((cells + 16, wide), full),
            pltpu.VMEM((3, high, 3 * wide), half),
            pltpu.VMEM((rows, tall + 16, thin), full),
            pltpu.VMEM((rows + 2, tall, 3 * thin), half),
            pltpu.VMEM((high, wide), half),
            pltpu.VMEM((rows, tall, thin), half),
            pltpu.VMEM((3, wide, 3 * wide), half),
            pltpu.VMEM((3, thin, 3 * thin), half),
            pltpu.VMEM((2, 3, va, 3 * wide), half),
            pltpu.VMEM((2, 3, vo, 3 * thin), half),
            pltpu.VMEM((3, va, 3 * wide), half),
            pltpu.VMEM((3, vo, 3 * thin), half),
            pltpu.VMEM((3, va, 3 * wide), half),
            pltpu.VMEM((3, vo, 3 * thin), half),
            pltpu.VMEM((samples, piece, 128), half),
            pltpu.VMEM((samples - 1, piece, 128), half),
            pltpu.SemaphoreType.DMA((2, 5 + samples)),
            pltpu.SemaphoreType.DMA((2, 10)),
        ],
        compiler_params=pltpu.CompilerParams(
            collective_id=0, has_side_effects=True, vmem_limit_bytes=48 * 1024 * 1024
        ),
    )(
        x.reshape(cells, wide),
        p.reshape(rows, lons, thin),
        wet,
        wa.reshape(3, 3 * wide, wide),
        wo.reshape(3, 3 * thin, thin),
        emit,
        drive,
        by_band(rid),
        by_band(rfac),
        tid.reshape(cells, -1).T,
        tfac.reshape(cells, -1).T,
        cota.reshape(cells, wide),
        coto.reshape(rows, lons, thin),
    )
    return outs[0].reshape(x.shape), outs[1].reshape(p.shape), outs[2], outs[3]


def per_device(*arrays):
    x, p = arrays[0], arrays[1]
    if (
        lax.axis_size("comp") == 4
        and x.shape[:2] == (1, 1)
        and p.shape[:2] == (1, 8)
        and x.shape[3] == 256
        and p.shape[3] == 128
        and p.shape[3] % (16 * lax.axis_size("dp")) == 0
    ):
        return whole_step(*arrays)
    return by_parts(*arrays)


def solution(mesh):
    placed = (
        P("dp", "comp", None, None),
        P("dp", None, "comp", None),
        P(None, "comp"),
        P(),
        P(),
        P(),
        P(),
        P("comp", None, None),
        P("comp", None, None),
        P("comp", None, None),
        P("comp", None, None),
        P("dp", "comp", None, None),
        P("dp", None, "comp", None),
    )
    return jax.shard_map(
        per_device,
        mesh=mesh,
        in_specs=placed,
        out_specs=(
            P("dp", "comp", None, None),
            P("dp", None, "comp", None),
            P(None, "dp", "comp"),
            P(None, "dp", "comp"),
        ),
        check_vma=False,
    )
```

```python
import functools

import jax
import jax.numpy as jnp
from jax import lax
from jax.experimental import pallas as pl
from jax.experimental.pallas import tpu as pltpu
from jax.sharding import PartitionSpec as P


def with_halo(cells, sides, width, closed):
    for axis, dim in sides:
        count = lax.axis_size(axis)
        ends = count if closed else count - 1
        head = lax.slice_in_dim(cells, 0, width, axis=dim)
        tail = lax.slice_in_dim(cells, cells.shape[dim] - width, cells.shape[dim], axis=dim)
        cells = jnp.concatenate(
            [
                lax.ppermute(tail, axis, [(i, (i + 1) % count) for i in range(ends)]),
                cells,
                lax.ppermute(head, axis, [((i + 1) % count, i) for i in range(ends)]),
            ],
            axis=dim,
        )
    return cells


def convolve(padded, kernel):
    sample_batch = padded.shape[0]
    rows = padded.shape[1] - 2
    cols = padded.shape[2] - 2
    width = padded.shape[3]
    total = jnp.zeros((sample_batch * rows * cols, kernel.shape[2]), jnp.float32)
    for tap_row in range(3):
        for tap_col in range(3):
            window = padded[:, tap_row : tap_row + rows, tap_col : tap_col + cols].reshape(
                -1, width
            )
            total = total + jnp.dot(
                window, kernel[3 * tap_row + tap_col], preferred_element_type=jnp.float32
            )
    return total.reshape(sample_batch, rows, cols, -1)


MESH = pl.DeviceIdType.MESH


def joined_terms(padded, delta):
    rows = padded.shape[1] - 2
    cols = padded.shape[2] - 2
    flat_delta = delta.reshape(-1, delta.shape[-1])
    joined = jnp.concatenate([padded[:, :, b : b + cols] for b in range(3)], axis=-1)
    return jnp.stack(
        [
            lax.dot_general(
                flat_delta,
                joined[:, a : a + rows].reshape(-1, joined.shape[-1]),
                (((0,), (0,)), ((), ())),
                preferred_element_type=jnp.float32,
            )
            for a in range(3)
        ]
    )


def remote(src, dst, sems, index, target):
    return pltpu.make_async_remote_copy(
        src_ref=src,
        dst_ref=dst,
        send_sem=sems.at[0, index],
        recv_sem=sems.at[1, index],
        device_id=target,
        device_id_type=MESH,
    )


def two_parts(value):
    high = value.astype(jnp.bfloat16)
    return high, (value - high.astype(jnp.float32)).astype(jnp.bfloat16)


def picked(ids, factors, first, cells):
    extent = cells.shape[0]
    place = lax.broadcasted_iota(jnp.int32, (extent, ids.shape[1]), 0) + first
    shares = jnp.zeros(place.shape, jnp.float32)
    for k in range(ids.shape[0]):
        shares = shares + jnp.where(place == ids[k : k + 1], factors[k : k + 1], 0.0)
    return sum(turned_dot(part, cells) for part in two_parts(shares))


def turned_dot(left, right):
    return lax.dot_general(
        left, right, (((0,), (0,)), ((), ())), preferred_element_type=jnp.float32
    )


def step_kernel(
    samples,
    x_ref, p_ref, wet_ref, wa_ref, wo_ref, emit_ref, drive_ref,
    rid_ref, rfac_ref, tid_ref, tfac_ref, cota_ref, coto_ref,
    nexta_ref, nexto_ref, outa_ref, outo_ref,
    hal, xo, fs, fi, hs, hr, ax, xca, pp, xco, dea, deo, ga_ref, go_ref,
    r1a, r1o, s2a, s2o, r2a, r2o, da, do, r4a, r4o, sems, near,
):
    comp = lax.axis_index("comp")
    dp = lax.axis_index("dp")
    bands = 4
    rows, lons = p_ref.shape[0], p_ref.shape[1]
    cells = x_ref.shape[0]
    core = lax.rem(comp, 2)
    half = comp // 2
    twin = {"comp": 2 * half + 1 - core}
    across = {"comp": 2 * (1 - half) + core}
    barrier = pltpu.get_barrier_semaphore()
    for k in range(1, bands):
        pl.semaphore_signal(
            barrier, inc=1, device_id={"comp": lax.rem(comp + k, bands)}, device_id_type=MESH
        )
    for k in range(1, samples):
        pl.semaphore_signal(
            barrier, inc=1, device_id={"dp": lax.rem(dp + k, samples)}, device_id_type=MESH
        )
    pl.semaphore_wait(barrier, samples + bands - 2)
    up = {"comp": lax.rem(comp + 1, bands)}
    down = {"comp": lax.rem(comp + bands - 1, bands)}
    halos = [
        remote(x_ref, hal.at[0], near, 0, up),
        remote(x_ref, hal.at[1], near, 1, down),
    ]
    swaps = []
    for k in range(1, bands):
        peer = lax.rem(comp + k, bands)
        swaps.append(
            remote(
                p_ref.at[pl.ds(2 * peer, 2)],
                xo.at[pl.ds(2 * comp, 2)],
                near,
                3 + k,
                {"comp": peer},
            )
        )
    for copy in halos + swaps:
        copy.start()
    pp[...] = jnp.zeros_like(pp)
    for r in range(rows):
        pp[r, 8 : 8 + lons, :] = p_ref[r].astype(jnp.float32)
    hs[0] = pp[:, 7 + lons : 8 + lons, :]
    hs[1] = pp[:, 8:9, :]
    sides = [remote(hs.at[0], hr.at[0], near, 2, up), remote(hs.at[1], hr.at[1], near, 3, down)]
    for copy in sides:
        copy.start()
    xo[pl.ds(2 * comp, 2)] = p_ref[pl.ds(2 * comp, 2)]
    wide = x_ref.shape[1]
    xca[...] = jnp.zeros_like(xca)
    dea[...] = jnp.zeros_like(dea)
    xco[...] = jnp.zeros_like(xco)
    deo[...] = jnp.zeros_like(deo)
    for a in (1, 0, 2):
        if a == 1:
            line = x_ref[...].astype(jnp.float32)
        else:
            halos[a // 2].wait_recv()
            line = jnp.where(
                comp == (0 if a == 0 else bands - 1), 0.0, hal[a // 2].astype(jnp.float32)
            )
        ax[8 : 8 + cells, :] = line
        ax[7:8, :] = line[cells - 1 : cells]
        ax[8 + cells : 9 + cells, :] = line[0:1]
        for b in range(3):
            xca[a, 0:cells, b * wide : (b + 1) * wide] = ax[7 + b : 7 + b + cells, :].astype(
                jnp.bfloat16
            )
    za = jnp.dot(xca[0], wa_ref[0], preferred_element_type=jnp.float32)
    za = za + jnp.dot(xca[1], wa_ref[1], preferred_element_type=jnp.float32)
    za = za + jnp.dot(xca[2], wa_ref[2], preferred_element_type=jnp.float32)
    za = za[:cells]
    for copy in swaps:
        copy.wait_recv()
    total_lons = lons * bands
    surface = jnp.zeros((cells, p_ref.shape[2]), jnp.float32)
    for t in range(bands):
        for r in range(2):
            surface = surface + picked(
                tid_ref[...],
                tfac_ref[...],
                (2 * comp + r) * total_lons + t * lons,
                xo[2 * t + r],
            )
    za = za + jnp.dot(
        surface.astype(jnp.bfloat16), drive_ref[...], preferred_element_type=jnp.float32
    )
    gate = lax.logistic(za)
    nexta_ref[...] = x_ref[...].astype(jnp.float32) + za * gate
    dea[0:cells, :] = (
        cota_ref[...].astype(jnp.float32) * (gate * (1.0 + za * (1.0 - gate)))
    ).astype(jnp.bfloat16)
    for a in range(3):
        ga_ref[a] = turned_dot(dea[...], xca[a]).astype(jnp.bfloat16)
    wa = s2a.shape[1]
    wo = s2o.shape[1]

    def block(ref, width, band):
        return ref.at[:, pl.ds(pl.multiple_of(band * width, width), width), :]

    first = []
    for n, side in enumerate((1 - half, half)):
        band = 2 * side + 1 - core
        first.append(
            (
                remote(block(ga_ref, wa, band), r1a.at[n], sems, 2 * n, twin),
                remote(block(go_ref, wo, band), r1o.at[n], sems, 2 * n + 1, twin),
            )
        )
    first[0][0].start()
    first[1][0].start()
    flux_cells = jnp.dot(
        x_ref[...], emit_ref[...], preferred_element_type=jnp.float32
    ).astype(jnp.bfloat16)
    for t in range(bands):
        for r in range(2):
            fs[2 * t + r] = picked(
                rid_ref[r, :, t * lons : (t + 1) * lons],
                rfac_ref[r, :, t * lons : (t + 1) * lons],
                comp * cells,
                flux_cells,
            ).astype(jnp.bfloat16)
    fluxes = []
    for k in range(1, bands):
        peer = lax.rem(comp + k, bands)
        copy = remote(
            fs.at[pl.ds(2 * peer, 2)],
            fi.at[pl.ds(2 * comp, 2)],
            near,
            6 + k,
            {"comp": peer},
        )
        copy.start()
        fluxes.append(copy)
    fi[pl.ds(2 * comp, 2)] = fs[pl.ds(2 * comp, 2)]
    for copy in sides:
        copy.wait_recv()
    pp[:, 7:8, :] = hr[0]
    pp[:, 8 + lons : 9 + lons, :] = hr[1]
    thin = p_ref.shape[2]

    def join(r, carry):
        for b in range(3):
            xco[r + 1, 0:lons, b * thin : (b + 1) * thin] = pp[
                r, 7 + b : 7 + b + lons, :
            ].astype(jnp.bfloat16)
        return carry

    lax.fori_loop(0, rows, join, 0)
    other = 2 * (1 - half) + core
    first[0][0].wait_recv()
    s2a[...] = (
        block(ga_ref, wa, other)[...].astype(jnp.float32) + r1a[0].astype(jnp.float32)
    ).astype(jnp.bfloat16)
    second_a = remote(s2a, r2a, sems, 4, across)
    second_a.start()
    for copy in fluxes:
        copy.wait_recv()

    def ocean(r, carry):
        zo = jnp.dot(xco[r], wo_ref[0], preferred_element_type=jnp.float32)
        zo = zo + jnp.dot(xco[r + 1], wo_ref[1], preferred_element_type=jnp.float32)
        zo = zo + jnp.dot(xco[r + 2], wo_ref[2], preferred_element_type=jnp.float32)
        zo = zo[:lons] + fi[r].astype(jnp.float32)
        chosen = jnp.where(
            lax.broadcasted_iota(jnp.int32, (rows, thin), 0) == r, 1.0, 0.0
        ).astype(jnp.bfloat16)
        wet = turned_dot(wet_ref[...].astype(jnp.float32).astype(jnp.bfloat16), chosen)
        gate = lax.logistic(zo)
        nexto_ref[r] = p_ref[r].astype(jnp.float32) + wet * (zo * gate)
        deo[r, 0:lons, :] = (
            coto_ref[r].astype(jnp.float32) * wet * (gate * (1.0 + zo * (1.0 - gate)))
        ).astype(jnp.bfloat16)
        return carry

    lax.fori_loop(0, rows, ocean, 0)
    first[1][0].wait_recv()
    own_a = block(ga_ref, wa, comp)[...].astype(jnp.float32) + r1a[1].astype(jnp.float32)
    second_a.wait_recv()
    own_a = own_a + r2a[...].astype(jnp.float32)
    ca = outa_ref.shape[1]
    co = outo_ref.shape[1]
    ta = own_a.reshape(3 * wa, -1)
    ta = jnp.concatenate([ta, jnp.zeros((wa, ta.shape[1]), jnp.float32)], axis=0).T
    ta = ta.astype(jnp.bfloat16)
    for d in range(samples):
        for b in range(3):
            piece = ta[(b * samples + d) * ca : (b * samples + d + 1) * ca]
            da[d, b * ca : (b + 1) * ca, :] = piece[:, :128]
            da[d, (3 + b) * ca : (4 + b) * ca, :] = piece[:, 128:]
    third_a = []
    for k in range(1, samples):
        peer = lax.rem(dp + k, samples)
        copy = remote(da.at[peer], r4a.at[k - 1], sems, 5 + k, {"dp": peer})
        copy.start()
        third_a.append(copy)
    delta = deo[...].reshape(-1, thin)
    for a in range(3):
        go_ref[a] = turned_dot(
            delta, xco[a : a + rows].reshape(-1, 3 * thin)
        ).astype(jnp.bfloat16)
    first[0][1].start()
    first[1][1].start()
    first[0][1].wait_recv()
    s2o[...] = (
        block(go_ref, wo, other)[...].astype(jnp.float32) + r1o[0].astype(jnp.float32)
    ).astype(jnp.bfloat16)
    second_o = remote(s2o, r2o, sems, 5, across)
    second_o.start()
    first[1][1].wait_recv()
    own_o = block(go_ref, wo, comp)[...].astype(jnp.float32) + r1o[1].astype(jnp.float32)
    second_o.wait_recv()
    own_o = own_o + r2o[...].astype(jnp.float32)
    to = own_o.reshape(3 * wo, -1)
    to = jnp.concatenate([to, jnp.zeros((wo, to.shape[1]), jnp.float32)], axis=0).T
    to = to.astype(jnp.bfloat16)
    for d in range(samples):
        for b in range(3):
            do[d, b * co : (b + 1) * co, :] = to[
                (b * samples + d) * co : (b * samples + d + 1) * co
            ]
    third_o = []
    for k in range(1, samples):
        peer = lax.rem(dp + k, samples)
        copy = remote(do.at[peer], r4o.at[k - 1], sems, 4 + samples + k, {"dp": peer})
        copy.start()
        third_o.append(copy)
    total = da[dp].astype(jnp.float32)
    for k in range(samples - 1):
        third_a[k].wait_recv()
        total = total + r4a[k].astype(jnp.float32)
    for a in range(3):
        for b in range(3):
            row = b * ca + (a // 2) * 3 * ca
            outa_ref[3 * a + b] = total[row : row + ca, (a % 2) * wa : (a % 2 + 1) * wa]
    total = do[dp].astype(jnp.float32)
    for k in range(samples - 1):
        third_o[k].wait_recv()
        total = total + r4o[k].astype(jnp.float32)
    for a in range(3):
        for b in range(3):
            outo_ref[3 * a + b] = total[b * co : (b + 1) * co, a * wo : (a + 1) * wo]
    for pair in first:
        for copy in pair:
            copy.wait_send()
    second_a.wait_send()
    second_o.wait_send()
    for copy in third_a + third_o:
        copy.wait_send()
    for copy in halos + swaps + sides + fluxes:
        copy.wait_send()


def plain_sum(joined):
    width = joined.shape[2] // 3
    terms = joined.reshape(3, -1, 3, width).transpose(0, 2, 3, 1).reshape(9, width, -1)
    banded = lax.psum_scatter(terms, "comp", scatter_dimension=2, tiled=True)
    return lax.psum_scatter(banded, "dp", scatter_dimension=1, tiled=True)


def silu_slope(value):
    logistic = jax.nn.sigmoid(value)
    return logistic * (1.0 + value * (1.0 - logistic))


def by_parts(
    climate_vector,
    pelagic_vector,
    wet_land_flags,
    sky_convolution_weights,
    pelagic_convolution_weights,
    interface_emission_map,
    thermal_drive_linear_map,
    regrid_donor_ids,
    regrid_donor_factors,
    thermal_donor_ids,
    thermal_donor_factors,
    upcoming_sky_sensitivity,
    upcoming_pelagic_sensitivity,
):
    sample_batch, band_rows, atmos_lons, atmos_width = climate_vector.shape
    ocean_rows, band_lons, ocean_grid_width = (
        pelagic_vector.shape[1],
        pelagic_vector.shape[2],
        pelagic_vector.shape[3],
    )
    bands = lax.axis_size("comp")
    parallel_slice = lax.axis_index("comp")
    coupled_entry_pairs = 2 * band_rows
    pelagic_east_total = band_lons * bands
    near = regrid_donor_ids.shape[2]
    ocean_blocks = pelagic_vector.reshape(
        sample_batch, bands, coupled_entry_pairs, band_lons, ocean_grid_width
    )
    surface_exchange_input = lax.all_to_all(
        ocean_blocks, "comp", split_axis=1, concat_axis=1, tiled=True
    )
    flux_cells = jnp.dot(
        climate_vector.reshape(-1, atmos_width),
        interface_emission_map,
        preferred_element_type=jnp.float32,
    )
    flux_cells = flux_cells.astype(jnp.bfloat16)
    cells_flat = flux_cells.reshape(sample_batch, band_rows * atmos_lons, ocean_grid_width)
    local_flux = regrid_donor_ids - parallel_slice * (band_rows * atmos_lons)
    local_flux = local_flux.reshape(coupled_entry_pairs, bands, band_lons, near).transpose(
        1, 0, 2, 3
    )
    flux_weights = regrid_donor_factors.reshape(
        coupled_entry_pairs, bands, band_lons, near
    ).transpose(1, 0, 2, 3)
    flux_taken = jnp.take(cells_flat, local_flux, axis=1).astype(jnp.float32)
    flux_send = jnp.sum(flux_taken * flux_weights[None, ..., None], axis=4).astype(jnp.bfloat16)
    flux_in = lax.all_to_all(flux_send, "comp", split_axis=1, concat_axis=1, tiled=True)
    padded_a = with_halo(climate_vector, (("comp", 1),), 1, False)
    padded_a = jnp.concatenate([padded_a[:, :, -1:], padded_a, padded_a[:, :, :1]], axis=2)
    conv_a = convolve(padded_a, sky_convolution_weights)
    padded_o = with_halo(pelagic_vector, (("comp", 2),), 1, True)
    padded_o = jnp.pad(padded_o, ((0, 0), (1, 1), (0, 0), (0, 0)))
    conv_o = convolve(padded_o, pelagic_convolution_weights)
    source_row_index = (
        thermal_donor_ids // pelagic_east_total - parallel_slice * coupled_entry_pairs
    )
    donor_east_ids = thermal_donor_ids % pelagic_east_total
    nearby_thermal_values = (
        donor_east_ids // band_lons * coupled_entry_pairs + source_row_index
    ) * band_lons + donor_east_ids % band_lons
    pelagic_picked_sites = jnp.take(
        surface_exchange_input.reshape(sample_batch, -1, ocean_grid_width),
        nearby_thermal_values,
        axis=1,
    ).astype(jnp.float32)
    interface_coupling_terms = jnp.sum(
        pelagic_picked_sites * thermal_donor_factors[None, ..., None], axis=3
    ).astype(jnp.bfloat16)
    atmosphere_forcing = jnp.dot(
        interface_coupling_terms.reshape(-1, ocean_grid_width),
        thermal_drive_linear_map,
        preferred_element_type=jnp.float32,
    )
    za = conv_a + atmosphere_forcing.reshape(sample_batch, band_rows, atmos_lons, atmos_width)
    atmos_next = climate_vector.astype(jnp.float32) + jax.nn.silu(za)
    flux_ocean = flux_in.reshape(sample_batch, ocean_rows, band_lons, ocean_grid_width)
    wet = wet_land_flags.astype(jnp.float32)[None, :, :, None]
    zo = conv_o + flux_ocean.astype(jnp.float32)
    ocean_next = pelagic_vector.astype(jnp.float32) + wet * jax.nn.silu(zo)
    delta_a = (upcoming_sky_sensitivity.astype(jnp.float32) * silu_slope(za)).astype(jnp.bfloat16)
    delta_o = (upcoming_pelagic_sensitivity.astype(jnp.float32) * wet * silu_slope(zo)).astype(
        jnp.bfloat16
    )
    summed = (
        plain_sum(joined_terms(padded_a, delta_a)),
        plain_sum(joined_terms(padded_o, delta_o)),
    )
    return (atmos_next, ocean_next, summed[0], summed[1])


def whole_step(x, p, wet, wa, wo, emit, drive, rid, rfac, tid, tfac, cota, coto):
    samples = lax.axis_size("dp")
    bands = lax.axis_size("comp")
    rows, lons, thin = p.shape[1:]
    cells, wide = x.shape[2:]
    ca, co, va, vo = wide // samples, thin // samples, wide // bands, thin // bands
    tall = -(-lons // 64) * 64
    high = -(-cells // 128) * 128

    vmem = pl.BlockSpec(memory_space=pltpu.VMEM)
    half, full = jnp.bfloat16, jnp.float32
    outs = pl.pallas_call(
        functools.partial(step_kernel, samples),
        out_shape=(
            jax.ShapeDtypeStruct((cells, wide), full),
            jax.ShapeDtypeStruct((rows, lons, thin), full),
            jax.ShapeDtypeStruct((9, ca, va), full),
            jax.ShapeDtypeStruct((9, co, vo), full),
        ),
        in_specs=[vmem] * 13,
        out_specs=(vmem,) * 4,
        scratch_shapes=[
            pltpu.VMEM((2, cells, wide), half),
            pltpu.VMEM((rows, lons, thin), half),
            pltpu.VMEM((2 * bands, lons, thin), half),
            pltpu.VMEM((rows, lons, thin), half),
            pltpu.VMEM((2, rows, 1, thin), full),
            pltpu.VMEM((2, rows, 1, thin), full),
            pltpu.VMEM((cells + 16, wide), full),
            pltpu.VMEM((3, high, 3 * wide), half),
            pltpu.VMEM((rows, tall + 16, thin), full),
            pltpu.VMEM((rows + 2, tall, 3 * thin), half),
            pltpu.VMEM((high, wide), half),
            pltpu.VMEM((rows, tall, thin), half),
            pltpu.VMEM((3, wide, 3 * wide), half),
            pltpu.VMEM((3, thin, 3 * thin), half),
            pltpu.VMEM((2, 3, va, 3 * wide), half),
            pltpu.VMEM((2, 3, vo, 3 * thin), half),
            pltpu.VMEM((3, va, 3 * wide), half),
            pltpu.VMEM((3, vo, 3 * thin), half),
            pltpu.VMEM((3, va, 3 * wide), half),
            pltpu.VMEM((3, vo, 3 * thin), half),
            pltpu.VMEM((samples, 6 * ca, 128), half),
            pltpu.VMEM((samples, 3 * co, 128), half),
            pltpu.VMEM((samples - 1, 6 * ca, 128), half),
            pltpu.VMEM((samples - 1, 3 * co, 128), half),
            pltpu.SemaphoreType.DMA((2, 4 + 2 * samples)),
            pltpu.SemaphoreType.DMA((2, 10)),
        ],
        compiler_params=pltpu.CompilerParams(
            collective_id=0, has_side_effects=True, vmem_limit_bytes=48 * 1024 * 1024
        ),
    )(
        x.reshape(cells, wide),
        p.reshape(rows, lons, thin),
        wet,
        wa.reshape(3, 3 * wide, wide),
        wo.reshape(3, 3 * thin, thin),
        emit,
        drive,
        rid.transpose(0, 2, 1),
        rfac.transpose(0, 2, 1),
        tid.reshape(cells, -1).T,
        tfac.reshape(cells, -1).T,
        cota.reshape(cells, wide),
        coto.reshape(rows, lons, thin),
    )
    return outs[0].reshape(x.shape), outs[1].reshape(p.shape), outs[2], outs[3]


def per_device(*arrays):
    x, p = arrays[0], arrays[1]
    if (
        lax.axis_size("comp") == 4
        and x.shape[:2] == (1, 1)
        and p.shape[:2] == (1, 8)
        and x.shape[3] == 256
        and p.shape[3] == 128
        and p.shape[3] % (16 * lax.axis_size("dp")) == 0
    ):
        return whole_step(*arrays)
    return by_parts(*arrays)


def solution(mesh):
    placed = (
        P("dp", "comp", None, None),
        P("dp", None, "comp", None),
        P(None, "comp"),
        P(),
        P(),
        P(),
        P(),
        P("comp", None, None),
        P("comp", None, None),
        P("comp", None, None),
        P("comp", None, None),
        P("dp", "comp", None, None),
        P("dp", None, "comp", None),
    )
    return jax.shard_map(
        per_device,
        mesh=mesh,
        in_specs=placed,
        out_specs=(
            P("dp", "comp", None, None),
            P("dp", None, "comp", None),
            P(None, "dp", "comp"),
            P(None, "dp", "comp"),
        ),
        check_vma=False,
    )
```
